32 devices in a mesh: fsdp: 4 (over x, core), seq: 8 (over z, y).
Axes of the slice: x: 2, y: 2, z: 4, core: 2. Of those that a mesh axis runs over, the one named last changes fastest.
Arguments:
- inputs: bfloat16 [96, 6144], P(('fsdp', 'seq')), may hold values from -6 to 6
- out_grad: bfloat16 [96, 6144], P(('fsdp', 'seq')), may hold values from -6 to 6
- first_tiles: bfloat16 [8, 208, 4096], P('seq', 'fsdp'), may hold values from -0.15625 to 0.15625
- first_count: int32 [8, 4], P('seq'), may hold values from 1 to 52, 192 in all within a row
- first_blocks: int32 [8, 192], P('seq'), may hold values from 0 to 767, as said below
- second_tiles: bfloat16 [8, 208, 4096], P('seq', 'fsdp'), may hold values from -0.109375 to 0.109375
- second_count: int32 [8, 4], P('seq'), may hold values from 1 to 52, 192 in all within a row
- second_blocks: int32 [8, 192], P('seq'), may hold values from 0 to 767, as said below
Outputs:
- output: bfloat16 [96, 6144], P(('fsdp', 'seq'))
- in_grad: bfloat16 [96, 6144], P(('fsdp', 'seq'))
The draws below stay inside these ranges and needn't reach their ends.
Inputs may be any that keep to these rules, and one draw needn't show every extreme that they name: Each row of first_blocks lists 192 different blocks of 0 to 767, and holds both 0 and 767. Each row of second_blocks lists 192 different blocks of 0 to 767, and holds both 0 and 767. `first_count`: each row sums to 192, and its largest count is 52. `second_count`: each row sums to 192, and its largest count is 52.
All inputs are finite; a program needn't handle non-finite values.
Results may differ from the reference program's by a relative error of at most 0.0051.
Values may be sent and summed in bfloat16 or wider, within the bound.
A program may use at most 128 MiB of HBM per device.

```python
import math
import jax
import jax.numpy as jnp
import numpy as np
from jax import lax

D = 6144
BS = 64
HB_DEV = 8
DB = 96
BLOCKS = 768
KEPT = 192
CAP = 52
ROWS = 96
N_FSDP = 4
N_SEQ = 8


def pick_blocks(key):
    keys = jax.random.split(key, N_SEQ)

    def one_row(row_key):
        order = jax.random.permutation(row_key, BLOCKS - 2).astype(jnp.int32) + 1
        low = jnp.zeros((1,), jnp.int32)
        high = jnp.full((1,), BLOCKS - 1, jnp.int32)
        return jnp.concatenate([low, order[:KEPT - 2], high])
    return jax.vmap(one_row)(keys)


def draw_first_blocks(key, part):
    return pick_blocks(jax.random.fold_in(key, 11))


def draw_second_blocks(key, part):
    return pick_blocks(jax.random.fold_in(key, 23))


def levels(rng, shape, pieces, smallest, top_value):
    gain, own = 1.0, jax.random.fold_in(rng, 6)
    for dim, parts in pieces:
        draws = jnp.exp(jax.random.uniform(jax.random.fold_in(own, dim), (parts,), jnp.float32, smallest / len(pieces), top_value / len(pieces)))
        gain = gain * jnp.repeat(draws, shape[dim] // parts).reshape([-1 if axis == dim else 1 for axis in range(len(shape))])
    return gain


def length_profile(number_of, total, most, lean):
    weights = [(1 << 20) // math.isqrt(grade ** lean) + 1 for grade in range(2, number_of + 1)]
    spare, holding = total - most - (number_of - 1), [1] * (number_of - 1)
    while spare > 0:
        candidates = [i for i in range(number_of - 1) if holding[i] < most]
        pool, budget = sum([weights[i] for i in candidates]), spare
        for i in candidates:
            addition = min(most - holding[i], max(1, budget * weights[i] // pool), spare)
            holding[i] = holding[i] + addition
            spare = spare - addition
    return np.array([most] + holding)


def uneven(own_key, number_of, total, limit, lean):
    if number_of == 2:
        one = jax.random.randint(own_key, (), max(1, total - limit), min(limit, total - 1) + 1)
        return jnp.stack([one, total - one])
    tallies = jnp.asarray(length_profile(number_of, total, limit, lean), jnp.int32)
    couples = (number_of - 1) // 2
    source_of, sink = tallies[1:1 + 2 * couples:2], tallies[2:2 + 2 * couples:2]
    margin = jnp.minimum(source_of - 1, limit - sink)
    shifted = jax.random.randint(jax.random.fold_in(own_key, 1), (couples,), 0, 1 << 20) % (margin + 1)
    tallies = tallies.at[1:1 + 2 * couples:2].set(source_of - shifted).at[2:2 + 2 * couples:2].set(sink + shifted)
    return tallies[jax.random.permutation(jax.random.fold_in(own_key, 2), number_of)]


def centred(own_key, shape, width, most, cuts=(), held_as=jnp.bfloat16):
    loudness = levels(own_key, shape, cuts, -0.22, 0.18) if cuts else 1.0
    entries = jax.random.normal(own_key, shape, jnp.float32) * width * loudness
    return jnp.minimum(jnp.maximum(entries, -most), most).astype(held_as)


def setup_inputs(seed: int = 0) -> dict:
    arg_keys = jax.random.split(jax.random.key(seed), 9)
    inputs = centred(arg_keys[0], (ROWS, D), 1.0, 6.0, ((0, 32),))
    out_grad = centred(arg_keys[1], (ROWS, D), 1.0, 6.0, ((0, 32),))
    first_tiles = centred(arg_keys[2], (N_SEQ, N_FSDP * CAP, BS * BS), (KEPT * BS // HB_DEV) ** -0.5, 0.15625, ((0, 8), (1, 4)))
    first_count = jax.vmap(lambda own: uneven(own, N_FSDP, KEPT, CAP, 1))(jax.random.split(arg_keys[3], N_SEQ)).reshape((N_SEQ, N_FSDP)).astype(jnp.int32)
    first_blocks = draw_first_blocks(jax.random.fold_in(arg_keys[8], 71), 0)
    second_tiles = centred(arg_keys[5], (N_SEQ, N_FSDP * CAP, BS * BS), (D // 2) ** -0.5, 0.109375, ((0, 8), (1, 4)))
    second_count = jax.vmap(lambda own: uneven(own, N_FSDP, KEPT, CAP, 1))(jax.random.split(arg_keys[6], N_SEQ)).reshape((N_SEQ, N_FSDP)).astype(jnp.int32)
    second_blocks = draw_second_blocks(jax.random.fold_in(arg_keys[8], 71), 0)
    return dict(inputs=inputs, out_grad=out_grad, first_tiles=first_tiles, first_count=first_count, first_blocks=first_blocks, second_tiles=second_tiles, second_count=second_count, second_blocks=second_blocks)


def gelu_pair(hidden):
    inner = 0.7978845608 * (hidden + 0.044715 * hidden * hidden * hidden)
    tangent = jnp.tanh(inner)
    value = 0.5 * hidden * (1.0 + tangent)
    slope = 0.5 * (1.0 + tangent) + 0.5 * hidden * (1.0 - tangent * tangent) * 0.7978845608 * (1.0 + 3.0 * 0.044715 * hidden * hidden)
    return value, slope


def slot_table(counts, kept, capacity):
    ends = jnp.cumsum(counts, dtype=jnp.int32)
    starts = ends - counts
    entry = jnp.arange(kept, dtype=jnp.int32)
    owner = jnp.sum((entry[:, None] >= ends[None, :]).astype(jnp.int32), axis=1, dtype=jnp.int32)
    onehot = (owner[:, None] == jnp.arange(counts.shape[0], dtype=jnp.int32)[None, :]).astype(jnp.int32)
    first = jnp.sum(onehot * starts[None, :], axis=1, dtype=jnp.int32)
    return (owner * capacity + entry - first).astype(jnp.int32)


def dense_slice(tiles, counts, blocks, lead, trail):
    kept = blocks.shape[0]
    capacity = tiles.shape[0] // counts.shape[0]
    slots = slot_table(counts, kept, capacity)
    chosen = tiles[slots].reshape(kept, BS, BS)
    grid = jnp.zeros((lead * trail, BS, BS), tiles.dtype).at[blocks].set(chosen)
    return grid.reshape(lead, trail, BS, BS).transpose(0, 2, 1, 3).reshape(lead * BS, trail * BS)


def reference(inputs, out_grad, first_tiles, first_count, first_blocks, second_tiles, second_count, second_blocks):
    def one_slice(carry, item):
        total_out, total_grad = carry
        tiles_one, count_one, blocks_one, tiles_two, count_two, blocks_two = item
        first = dense_slice(tiles_one, count_one, blocks_one, DB, HB_DEV)
        second = dense_slice(tiles_two, count_two, blocks_two, HB_DEV, DB)
        hidden = jnp.dot(inputs, first, preferred_element_type=jnp.float32)
        value, slope = gelu_pair(hidden)
        acts = value.astype(jnp.bfloat16)
        total_out = total_out + jnp.dot(acts, second, preferred_element_type=jnp.float32)
        back = jnp.dot(out_grad, second.T, preferred_element_type=jnp.float32)
        pre_grad = (back * slope).astype(jnp.bfloat16)
        total_grad = total_grad + jnp.dot(pre_grad, first.T, preferred_element_type=jnp.float32)
        return (total_out, total_grad), None

    start = (jnp.zeros(inputs.shape, jnp.float32), jnp.zeros(inputs.shape, jnp.float32))
    (total_out, total_grad), unused = lax.scan(one_slice, start, (first_tiles, first_count, first_blocks, second_tiles, second_count, second_blocks))
    return total_out.astype(jnp.bfloat16), total_grad.astype(jnp.bfloat16)
```

```python
import functools

import jax
import jax.numpy as jnp
from jax import lax
from jax.experimental import pallas as pl
from jax.experimental.pallas import tpu as pltpu
from jax.sharding import PartitionSpec as P

BS = 64
HB_DEV = 8
HALF = BS // 2
LANES = 128
MESH = pl.DeviceIdType.MESH
F32 = jnp.float32
BF16 = jnp.bfloat16


def gelu_pair(hidden):
    inner = 0.7978845608 * (hidden + 0.044715 * hidden * hidden * hidden)
    tangent = jnp.tanh(inner)
    value = 0.5 * hidden * (1.0 + tangent)
    slope = 0.5 * (1.0 + tangent) + 0.5 * hidden * (1.0 - tangent * tangent) * 0.7978845608 * (
        1.0 + 3.0 * 0.044715 * hidden * hidden
    )
    return (value, slope)


def block_slots(counts, blocks, capacity, number):
    shards = counts.shape[1]
    kept = blocks.shape[1]
    zero = shards * capacity
    shard = jnp.arange(shards, dtype=jnp.int32)
    ends = jnp.sum(jnp.where(shard[:, None] <= shard[None, :], counts[:, :, None], 0), axis=1)
    entry = jnp.arange(kept, dtype=jnp.int32)
    past = entry[None, :, None] >= ends[:, None, :]
    slot = entry[None, :] + jnp.sum(jnp.where(past, capacity - counts[:, None, :], 0), axis=2)
    block = jnp.arange(number, dtype=jnp.int32)
    same = blocks[:, None, :] == block[None, :, None]
    return zero + jnp.sum(jnp.where(same, slot[:, None, :] - zero, 0), axis=2)


def natural(position):
    within = position % BS
    return position - within + 2 * (within % HALF) + within // HALF


def kernel(
    n_fsdp,
    n_seq,
    slots_ref,
    x_ref,
    g_ref,
    one_ref,
    two_ref,
    out_ref,
    grad_ref,
    tiles_one,
    tiles_two,
    stage,
    first,
    second,
    own_rows,
    got_x,
    got_g,
    spread,
    mat_x,
    mat_g,
    send_out,
    send_grad,
    got_out,
    got_grad,
    tile_send,
    tile_recv,
    row_send,
    row_recv,
    sum_send,
    sum_recv,
):
    capacity = one_ref.shape[1]
    own, width = x_ref.shape
    groups = width // LANES
    rows = own * n_seq
    chunk = own * groups
    width_blocks = width // BS
    hid = HB_DEV * BS
    zero_slot = n_fsdp * capacity
    f = lax.axis_index("fsdp")
    s = lax.axis_index("seq")
    pair = f + 1 - 2 * lax.rem(f, 2)
    others = [lax.rem(f + 2 * j, n_fsdp) for j in range(1, n_fsdp // 2)]
    pair_others = [lax.rem(pair + 2 * j, n_fsdp) for j in range(1, n_fsdp // 2)]
    peers = [lax.rem(s + j, n_seq) for j in range(1, n_seq)]

    barrier = pltpu.get_barrier_semaphore()
    for peer in [pair] + others:
        pl.semaphore_signal(barrier, inc=1, device_id=(peer, s), device_id_type=MESH)
    for peer in peers:
        pl.semaphore_signal(barrier, inc=1, device_id=(f, peer), device_id_type=MESH)

    def lay_tiles(source, target):
        for j in range(HALF):
            piece = source[0, :, j * LANES:(j + 1) * LANES].astype(F32)
            stage[pl.ds(j, capacity, stride=HALF), :] = piece
        target[pl.ds(f * capacity, capacity)] = (
            stage[0:capacity * HALF, :].astype(BF16).reshape(capacity, HALF, LANES)
        )
        target[zero_slot] = jnp.zeros((HALF, LANES), BF16)

    def tile_copy(which, buffer, owner, target, sem):
        part = buffer.at[pl.ds(owner * capacity, capacity)]
        return pltpu.make_async_remote_copy(
            src_ref=part,
            dst_ref=part,
            send_sem=tile_send.at[which, sem],
            recv_sem=tile_recv.at[which, owner],
            device_id=(target, s),
            device_id_type=MESH,
        )

    def row_copy(which, source, got, owner, target, sem):
        return pltpu.make_async_remote_copy(
            src_ref=source,
            dst_ref=got.at[owner],
            send_sem=row_send.at[which, sem],
            recv_sem=row_recv.at[which, owner],
            device_id=(f, target),
            device_id_type=MESH,
        )

    def sum_copy(which, source, got, owner, target, sem):
        return pltpu.make_async_remote_copy(
            src_ref=source.at[target],
            dst_ref=got.at[owner],
            send_sem=sum_send.at[which, sem],
            recv_sem=sum_recv.at[which, owner],
            device_id=(f, target),
            device_id_type=MESH,
        )

    sent = []

    def start(copy):
        copy.start()
        sent.append(copy)

    position = lax.broadcasted_iota(jnp.int32, (LANES, LANES), 1)
    row = lax.broadcasted_iota(jnp.int32, (LANES, LANES), 0)
    to_halves = jnp.where(natural(position) == row, 1.0, 0.0).astype(BF16)
    from_halves = jnp.where(natural(row) == position, 1.0, 0.0).astype(BF16)

    lay_tiles(one_ref, tiles_one)
    pl.semaphore_wait(barrier, 1 + len(others) + len(peers))
    for j, peer in enumerate(others):
        start(tile_copy(0, tiles_one, f, peer, j))

    def lay_rows(source):
        for k in range(groups):
            piece = source[:, k * LANES:(k + 1) * LANES].astype(F32)
            stage[pl.ds(k, own, stride=groups), :] = piece
        return stage[0:chunk, :].astype(BF16)

    own_rows[0] = jnp.dot(lay_rows(x_ref), to_halves, preferred_element_type=F32).astype(BF16)
    for j, peer in enumerate(peers):
        start(row_copy(0, own_rows.at[0], got_x, s, peer, j))
    start(tile_copy(0, tiles_one, f, pair, n_fsdp))
    lay_tiles(two_ref, tiles_two)
    for j, peer in enumerate(others):
        start(tile_copy(1, tiles_two, f, peer, j))
    own_rows[1] = lay_rows(g_ref)
    for j, peer in enumerate(peers):
        start(row_copy(1, own_rows.at[1], got_g, s, peer, j))
    start(tile_copy(1, tiles_two, f, pair, n_fsdp))
    got_x[s] = own_rows[0]
    got_g[s] = own_rows[1]

    def collect_rows(which, got, mat):
        for peer in peers:
            row_copy(which, own_rows.at[which], got, peer, peer, 0).wait_recv()
        spread[...] = got[...].reshape(n_seq * chunk, LANES).astype(F32)
        for k in range(groups):
            piece = spread[pl.ds(k, rows, stride=groups), :]
            mat[:, k * LANES:(k + 1) * LANES] = piece.astype(BF16)

    def collect_tiles(which, buffer):
        for j, peer in enumerate(others):
            tile_copy(which, buffer, peer, pair, 0).wait_recv()
            start(tile_copy(which, buffer, peer, pair, n_fsdp + 1 + j))
        tile_copy(which, buffer, pair, pair, 0).wait_recv()
        for peer in pair_others:
            tile_copy(which, buffer, peer, pair, 0).wait_recv()

    def joined(buffer, left, right):
        a = buffer[left]
        b = buffer[right]
        even = jnp.concatenate([a[:, :BS], b[:, :BS]], axis=1)
        odd = jnp.concatenate([a[:, BS:], b[:, BS:]], axis=1)
        return jnp.concatenate([even, odd], axis=0)

    collect_rows(0, got_x, mat_x)
    collect_tiles(0, tiles_one)

    step = 4

    def build_first(i, total):
        for r in range(step):
            block = (i * step + r) * HB_DEV
            at = pl.ds(pl.multiple_of((i * step + r) * BS, BS), BS)
            for j in range(HB_DEV // 2):
                tile = joined(
                    tiles_one, slots_ref[0, block + 2 * j], slots_ref[0, block + 2 * j + 1]
                )
                first[at, j * LANES:(j + 1) * LANES] = tile
        at = pl.ds(pl.multiple_of(i * (step * BS), step * BS), step * BS)
        return total + jnp.dot(mat_x[:, at], first[at, :], preferred_element_type=F32)

    hidden = lax.fori_loop(
        0, width_blocks // step, build_first, jnp.zeros((rows, hid), F32)
    )

    def reorder(value, matrix):
        parts = [
            jnp.dot(value[:, k * LANES:(k + 1) * LANES], matrix, preferred_element_type=F32)
            for k in range(hid // LANES)
        ]
        return jnp.concatenate(parts, axis=1)

    top = hidden.astype(BF16)
    rest = (hidden - top.astype(F32)).astype(BF16)
    hidden = reorder(top, to_halves) + reorder(rest, to_halves)
    value, slope = gelu_pair(hidden)
    acts = value.astype(BF16)

    collect_rows(1, got_g, mat_g)
    collect_tiles(1, tiles_two)

    def build_second(i, total):
        for k in range(2):
            block = i * 4 + 2 * k
            at = pl.ds(pl.multiple_of((2 * i + k) * LANES, LANES), LANES)
            for r in range(HB_DEV):
                left = r * width_blocks + block
                tile = joined(tiles_two, slots_ref[1, left], slots_ref[1, left + 1])
                second[r * BS:(r + 1) * BS, at] = tile
        at = pl.ds(pl.multiple_of(2 * i * LANES, 2 * LANES), 2 * LANES)
        weight = second[:, at]
        part = jnp.dot(acts, weight, preferred_element_type=F32)
        for k in range(2):
            spread[pl.ds(2 * i + k, rows, stride=groups), :] = part[:, k * LANES:(k + 1) * LANES]
        return total + lax.dot_general(
            mat_g[:, at], weight, (((1,), (1,)), ((), ())), preferred_element_type=F32
        )

    back = lax.fori_loop(0, groups // 2, build_second, jnp.zeros((rows, hid), F32))
    send_out[...] = spread[...].astype(BF16).reshape(n_seq, chunk, LANES)
    for j, peer in enumerate(peers):
        start(sum_copy(0, send_out, got_out, s, peer, j))

    pre = (back * slope).astype(BF16)
    pre = reorder(pre, from_halves).astype(BF16)

    def in_grad(i, carry):
        at = pl.ds(pl.multiple_of(2 * i * LANES, 2 * LANES), 2 * LANES)
        part = lax.dot_general(
            pre, first[at, :], (((1,), (1,)), ((), ())), preferred_element_type=F32
        )
        for k in range(2):
            spread[pl.ds(2 * i + k, rows, stride=groups), :] = part[:, k * LANES:(k + 1) * LANES]
        return carry

    lax.fori_loop(0, groups // 2, in_grad, 0)
    send_grad[...] = spread[...].astype(BF16).reshape(n_seq, chunk, LANES)
    for j, peer in enumerate(peers):
        start(sum_copy(1, send_grad, got_grad, s, peer, j))

    def finish(which, source, got, target):
        got[s] = source[s]
        for peer in peers:
            sum_copy(which, source, got, peer, peer, 0).wait_recv()
        total = lax.fori_loop(
            0, n_seq, lambda i, t: t + got[i].astype(F32), jnp.zeros((chunk, LANES), F32)
        )
        if which == 1:
            total = jnp.dot(total.astype(BF16), from_halves, preferred_element_type=F32)
        stage[0:chunk, :] = total
        for k in range(groups):
            piece = stage[pl.ds(k, own, stride=groups), :]
            target[:, k * LANES:(k + 1) * LANES] = piece.astype(BF16)

    finish(0, send_out, got_out, out_ref)
    finish(1, send_grad, got_grad, grad_ref)
    for copy in sent:
        copy.wait_send()


def on_device(
    n_fsdp,
    n_seq,
    inputs,
    out_grad,
    first_tiles,
    first_count,
    first_blocks,
    second_tiles,
    second_count,
    second_blocks,
):
    own, width = inputs.shape
    capacity = first_tiles.shape[1]
    width_blocks = width // BS
    rows = own * n_seq
    chunk = own * (width // LANES)
    hid = HB_DEV * BS
    table = block_slots(
        jnp.concatenate([first_count, second_count]),
        jnp.concatenate([first_blocks, second_blocks]),
        capacity,
        width_blocks * HB_DEV,
    )
    vmem = pl.BlockSpec(memory_space=pltpu.VMEM)
    bank = pltpu.VMEM((n_fsdp * capacity + 1, HALF, LANES), BF16)
    every = pltpu.VMEM((n_seq, chunk, LANES), BF16)
    return pl.pallas_call(
        functools.partial(kernel, n_fsdp, n_seq),
        out_shape=(
            jax.ShapeDtypeStruct((own, width), BF16),
            jax.ShapeDtypeStruct((own, width), BF16),
        ),
        in_specs=[pl.BlockSpec(memory_space=pltpu.SMEM)] + [vmem] * 4,
        out_specs=(vmem, vmem),
        scratch_shapes=[
            bank,
            bank,
            pltpu.VMEM((max(capacity * HALF, chunk), LANES), F32),
            pltpu.VMEM((width, hid), BF16),
            pltpu.VMEM((hid, width), BF16),
            pltpu.VMEM((2, chunk, LANES), BF16),
            every,
            every,
            pltpu.VMEM((n_seq * chunk, LANES), F32),
            pltpu.VMEM((rows, width), BF16),
            pltpu.VMEM((rows, width), BF16),
            every,
            every,
            every,
            every,
            pltpu.SemaphoreType.DMA((2, n_fsdp + n_fsdp // 2)),
            pltpu.SemaphoreType.DMA((2, n_fsdp)),
            pltpu.SemaphoreType.DMA((2, n_seq)),
            pltpu.SemaphoreType.DMA((2, n_seq)),
            pltpu.SemaphoreType.DMA((2, n_seq)),
            pltpu.SemaphoreType.DMA((2, n_seq)),
        ],
        compiler_params=pltpu.CompilerParams(
            collective_id=0, has_side_effects=True, vmem_limit_bytes=56 * 1024 * 1024
        ),
    )(table, inputs, out_grad, first_tiles, second_tiles)


def solution(mesh):
    placed = (
        P(("fsdp", "seq"), None),
        P(("fsdp", "seq"), None),
        P("seq", "fsdp", None),
        P("seq", None),
        P("seq", None),
        P("seq", "fsdp", None),
        P("seq", None),
        P("seq", None),
    )
    return jax.shard_map(
        functools.partial(on_device, mesh.shape["fsdp"], mesh.shape["seq"]),
        mesh=mesh,
        in_specs=placed,
        out_specs=(P(("fsdp", "seq"), None), P(("fsdp", "seq"), None)),
        check_vma=False,
    )
```

```python
import functools

import jax
import jax.numpy as jnp
from jax import lax
from jax.experimental import pallas as pl
from jax.experimental.pallas import tpu as pltpu
from jax.sharding import PartitionSpec as P

BS = 64
HB_DEV = 8
HALF = BS // 2
PARTS = 3
LANES = 128
MESH = pl.DeviceIdType.MESH
F32 = jnp.float32
BF16 = jnp.bfloat16


def gelu_pair(hidden):
    inner = 0.7978845608 * (hidden + 0.044715 * hidden * hidden * hidden)
    tangent = jnp.tanh(inner)
    value = 0.5 * hidden * (1.0 + tangent)
    slope = 0.5 * (1.0 + tangent) + 0.5 * hidden * (1.0 - tangent * tangent) * 0.7978845608 * (
        1.0 + 3.0 * 0.044715 * hidden * hidden
    )
    return (value, slope)


def block_slots(counts, blocks, capacity, number):
    shards = counts.shape[1]
    kept = blocks.shape[1]
    zero = shards * capacity
    shard = jnp.arange(shards, dtype=jnp.int32)
    ends = jnp.sum(jnp.where(shard[:, None] <= shard[None, :], counts[:, :, None], 0), axis=1)
    entry = jnp.arange(kept, dtype=jnp.int32)
    past = entry[None, :, None] >= ends[:, None, :]
    slot = entry[None, :] + jnp.sum(jnp.where(past, capacity - counts[:, None, :], 0), axis=2)
    block = jnp.arange(number, dtype=jnp.int32)
    same = blocks[:, None, :] == block[None, :, None]
    return zero + jnp.sum(jnp.where(same, slot[:, None, :] - zero, 0), axis=2)


def natural(position):
    within = position % BS
    return position - within + 2 * (within % HALF) + within // HALF


def kernel(
    n_fsdp,
    n_seq,
    slots_ref,
    x_ref,
    g_ref,
    one_ref,
    two_ref,
    out_ref,
    grad_ref,
    tiles_one,
    tiles_two,
    stage,
    first,
    second,
    own_rows,
    got_x,
    got_g,
    pair_x,
    pair_g,
    spread,
    mat_x,
    mat_g,
    sums_a,
    sums_b,
    pair_sums,
    send_sums,
    got_sums,
    tile_send,
    tile_recv,
    row_send,
    row_recv,
    share_send,
    share_recv,
    join_send,
    join_recv,
    sum_send,
    sum_recv,
):
    capacity = one_ref.shape[1]
    own, width = x_ref.shape
    groups = width // LANES
    rows = own * n_seq
    chunk = own * groups
    width_blocks = width // BS
    mine = HB_DEV // 2
    hid = mine * BS
    part_groups = groups // PARTS
    part_rows = rows * part_groups
    zero_slot = n_fsdp * capacity
    f = lax.axis_index("fsdp")
    s = lax.axis_index("seq")
    core = lax.rem(f, 2)
    pair = f + 1 - 2 * core
    others = [lax.rem(f + 2 * j, n_fsdp) for j in range(1, n_fsdp // 2)]
    pair_others = [lax.rem(pair + 2 * j, n_fsdp) for j in range(1, n_fsdp // 2)]
    peers = [lax.rem(s + j, n_seq) for j in range(1, n_seq)]

    barrier = pltpu.get_barrier_semaphore()
    for peer in [pair] + others:
        pl.semaphore_signal(barrier, inc=1, device_id=(peer, s), device_id_type=MESH)
    for peer in peers:
        pl.semaphore_signal(barrier, inc=1, device_id=(f, peer), device_id_type=MESH)

    def lay_tiles(source, target):
        for j in range(HALF):
            piece = source[0, :, j * LANES:(j + 1) * LANES].astype(F32)
            stage[pl.ds(j, capacity, stride=HALF), :] = piece
        target[pl.ds(f * capacity, capacity)] = (
            stage[0:capacity * HALF, :].astype(BF16).reshape(capacity, HALF, LANES)
        )
        target[zero_slot] = jnp.zeros((HALF, LANES), BF16)

    def tile_copy(which, buffer, owner, target, sem):
        part = buffer.at[pl.ds(owner * capacity, capacity)]
        return pltpu.make_async_remote_copy(
            src_ref=part,
            dst_ref=part,
            send_sem=tile_send.at[which, sem],
            recv_sem=tile_recv.at[which, owner],
            device_id=(target, s),
            device_id_type=MESH,
        )

    def row_copy(which, source, got, owner, target, sem):
        return pltpu.make_async_remote_copy(
            src_ref=source,
            dst_ref=got.at[owner],
            send_sem=row_send.at[which, sem],
            recv_sem=row_recv.at[which, owner],
            device_id=(f, target),
            device_id_type=MESH,
        )

    def sum_copy(turn, owner, target, sem):
        return pltpu.make_async_remote_copy(
            src_ref=send_sums.at[turn, target],
            dst_ref=got_sums.at[turn, owner],
            send_sem=sum_send.at[turn, sem],
            recv_sem=sum_recv.at[turn, owner],
            device_id=(f, target),
            device_id_type=MESH,
        )

    def share_copy(which, source, target):
        return pltpu.make_async_remote_copy(
            src_ref=source,
            dst_ref=target,
            send_sem=share_send.at[which],
            recv_sem=share_recv.at[which],
            device_id=(pair, s),
            device_id_type=MESH,
        )

    def join_copy(turn):
        return pltpu.make_async_remote_copy(
            src_ref=(sums_a, sums_b)[turn % 2].at[pl.ds(part_rows, part_rows)],
            dst_ref=pair_sums.at[turn],
            send_sem=join_send.at[turn],
            recv_sem=join_recv.at[turn],
            device_id=(pair, s),
            device_id_type=MESH,
        )

    sent = []

    def start(copy):
        copy.start()
        sent.append(copy)

    position = lax.broadcasted_iota(jnp.int32, (LANES, LANES), 1)
    row = lax.broadcasted_iota(jnp.int32, (LANES, LANES), 0)
    to_halves = jnp.where(natural(position) == row, 1.0, 0.0).astype(BF16)
    from_halves = jnp.where(natural(row) == position, 1.0, 0.0).astype(BF16)

    lay_tiles(one_ref, tiles_one)
    pl.semaphore_wait(barrier, 1 + len(others) + len(peers))
    for j, peer in enumerate(others):
        start(tile_copy(0, tiles_one, f, peer, j))

    def lay_rows(source):
        for k in range(groups):
            piece = source[:, k * LANES:(k + 1) * LANES].astype(F32)
            stage[pl.ds(k, own, stride=groups), :] = piece
        return stage[0:chunk, :].astype(BF16)

    own_rows[0] = jnp.dot(lay_rows(x_ref), to_halves, preferred_element_type=F32).astype(BF16)
    for j, peer in enumerate(peers):
        start(row_copy(0, own_rows.at[0], got_x, s, peer, j))
    start(tile_copy(0, tiles_one, f, pair, n_fsdp))
    lay_tiles(two_ref, tiles_two)
    for j, peer in enumerate(others):
        start(tile_copy(1, tiles_two, f, peer, j))
    own_rows[1] = lay_rows(g_ref)
    for j, peer in enumerate(peers):
        start(row_copy(1, own_rows.at[1], got_g, s, peer, j))
    start(tile_copy(1, tiles_two, f, pair, n_fsdp))
    got_x[s] = own_rows[0]
    got_g[s] = own_rows[1]

    def collect_rows(which, got, shared, mat):
        for peer in peers:
            row_copy(which, own_rows.at[which], got, peer, peer, 0).wait_recv()
        start(share_copy(which, got, shared))
        for half, source in enumerate((got, shared)):
            if half == 1:
                share_copy(which, got, shared).wait_recv()
            spread[...] = source[...].reshape(n_seq * chunk, LANES).astype(F32)
            for k in range(groups):
                piece = spread[pl.ds(k, rows, stride=groups), :]
                mat[half, :, k * LANES:(k + 1) * LANES] = piece.astype(BF16)

    def rows_of(mat, at):
        return jnp.concatenate([mat[0, :, at], mat[1, :, at]], axis=0)

    def collect_tiles(which, buffer):
        for j, peer in enumerate(others):
            tile_copy(which, buffer, peer, pair, 0).wait_recv()
            start(tile_copy(which, buffer, peer, pair, n_fsdp + 1 + j))
        tile_copy(which, buffer, pair, pair, 0).wait_recv()
        for peer in pair_others:
            tile_copy(which, buffer, peer, pair, 0).wait_recv()

    def joined(buffer, left, right):
        a = buffer[left]
        b = buffer[right]
        even = jnp.concatenate([a[:, :BS], b[:, :BS]], axis=1)
        odd = jnp.concatenate([a[:, BS:], b[:, BS:]], axis=1)
        return jnp.concatenate([even, odd], axis=0)

    collect_rows(0, got_x, pair_x, mat_x)
    collect_tiles(0, tiles_one)

    step = 4

    def build_first(i, total):
        for r in range(step):
            block = (i * step + r) * HB_DEV + core * mine
            at = pl.ds(pl.multiple_of((i * step + r) * BS, BS), BS)
            for j in range(mine // 2):
                tile = joined(
                    tiles_one, slots_ref[0, block + 2 * j], slots_ref[0, block + 2 * j + 1]
                )
                first[at, j * LANES:(j + 1) * LANES] = tile
        at = pl.ds(pl.multiple_of(i * (step * BS), step * BS), step * BS)
        return total + jnp.dot(rows_of(mat_x, at), first[at, :], preferred_element_type=F32)

    hidden = lax.fori_loop(
        0, width_blocks // step, build_first, jnp.zeros((2 * rows, hid), F32)
    )

    def reorder(value, matrix):
        parts = [
            jnp.dot(value[:, k * LANES:(k + 1) * LANES], matrix, preferred_element_type=F32)
            for k in range(hid // LANES)
        ]
        return jnp.concatenate(parts, axis=1)

    top = hidden.astype(BF16)
    rest = (hidden - top.astype(F32)).astype(BF16)
    hidden = reorder(top, to_halves) + reorder(rest, to_halves)
    value, slope = gelu_pair(hidden)
    acts = value.astype(BF16)

    collect_rows(1, got_g, pair_g, mat_g)
    collect_tiles(1, tiles_two)

    def pass_on(turn):
        join_copy(turn).wait_recv()
        kept = (sums_a, sums_b)[turn % 2][0:part_rows, :]
        total = (kept + pair_sums[turn]).astype(BF16)
        send_sums[turn] = total.reshape(n_seq, own * part_groups, LANES)
        for j, peer in enumerate(peers):
            start(sum_copy(turn, s, peer, j))

    pairs = part_groups // 2

    def columns(part, i):
        return pl.ds(pl.multiple_of((part * pairs + i) * 2 * LANES, 2 * LANES), 2 * LANES)

    def put(turn, i, value):
        target = (sums_a, sums_b)[turn % 2]
        for k in range(2):
            at = pl.ds(2 * i + k, 2 * rows, stride=part_groups)
            target[at, :] = value[:, k * LANES:(k + 1) * LANES]

    back = jnp.zeros((2 * rows, hid), F32)
    for turn in range(PARTS):
        if turn >= 2:
            join_copy(turn - 2).wait_send()

        def build_second(i, total):
            for k in range(2):
                block = ((turn * pairs + i) * 2 + k) * 2
                at = pl.ds(pl.multiple_of(block * BS, LANES), LANES)
                for r in range(mine):
                    left = (core * mine + r) * width_blocks + block
                    tile = joined(tiles_two, slots_ref[1, left], slots_ref[1, left + 1])
                    second[r * BS:(r + 1) * BS, at] = tile
            at = columns(turn, i)
            weight = second[:, at]
            put(turn, i, jnp.dot(acts, weight, preferred_element_type=F32))
            return total + lax.dot_general(
                rows_of(mat_g, at),
                weight,
                (((1,), (1,)), ((), ())),
                preferred_element_type=F32,
            )

        back = lax.fori_loop(0, pairs, build_second, back)
        join_copy(turn).start()
        if turn >= 1:
            pass_on(turn - 1)

    pre = (back * slope).astype(BF16)
    pre = reorder(pre, from_halves).astype(BF16)
    pass_on(PARTS - 1)

    for turn in range(PARTS, 2 * PARTS):
        join_copy(turn - 2).wait_send()

        def in_grad(i, carry):
            part = lax.dot_general(
                pre,
                first[columns(turn - PARTS, i), :],
                (((1,), (1,)), ((), ())),
                preferred_element_type=F32,
            )
            put(turn, i, part)
            return carry

        lax.fori_loop(0, pairs, in_grad, 0)
        join_copy(turn).start()
        if turn > PARTS:
            pass_on(turn - 1)
    pass_on(2 * PARTS - 1)

    part_chunk = own * part_groups
    for turn in range(2 * PARTS):
        for peer in peers:
            sum_copy(turn, peer, peer, 0).wait_recv()
        total = send_sums[turn, s].astype(F32)
        got_sums[turn, s] = jnp.zeros((part_chunk, LANES), BF16)
        total = lax.fori_loop(0, n_seq, lambda i, t: t + got_sums[turn, i].astype(F32), total)
        if turn >= PARTS:
            total = jnp.dot(total.astype(BF16), from_halves, preferred_element_type=F32)
        stage[0:part_chunk, :] = total
        target = out_ref if turn < PARTS else grad_ref
        for k in range(part_groups):
            piece = stage[pl.ds(k, own, stride=part_groups), :]
            column = (turn % PARTS) * part_groups + k
            target[:, column * LANES:(column + 1) * LANES] = piece.astype(BF16)
    for turn in range(2 * PARTS - 2, 2 * PARTS):
        join_copy(turn).wait_send()
    for copy in sent:
        copy.wait_send()


def on_device(
    n_fsdp,
    n_seq,
    inputs,
    out_grad,
    first_tiles,
    first_count,
    first_blocks,
    second_tiles,
    second_count,
    second_blocks,
):
    own, width = inputs.shape
    capacity = first_tiles.shape[1]
    width_blocks = width // BS
    rows = own * n_seq
    chunk = own * (width // LANES)
    hid = HB_DEV // 2 * BS
    part = rows * (width // LANES) // PARTS
    table = block_slots(
        jnp.concatenate([first_count, second_count]),
        jnp.concatenate([first_blocks, second_blocks]),
        capacity,
        width_blocks * HB_DEV,
    )
    vmem = pl.BlockSpec(memory_space=pltpu.VMEM)
    bank = pltpu.VMEM((n_fsdp * capacity + 1, HALF, LANES), BF16)
    every = pltpu.VMEM((n_seq, chunk, LANES), BF16)
    return pl.pallas_call(
        functools.partial(kernel, n_fsdp, n_seq),
        out_shape=(
            jax.ShapeDtypeStruct((own, width), BF16),
            jax.ShapeDtypeStruct((own, width), BF16),
        ),
        in_specs=[pl.BlockSpec(memory_space=pltpu.SMEM)] + [vmem] * 4,
        out_specs=(vmem, vmem),
        scratch_shapes=[
            bank,
            bank,
            pltpu.VMEM((max(capacity * HALF, chunk), LANES), F32),
            pltpu.VMEM((width, hid), BF16),
            pltpu.VMEM((hid, width), BF16),
            pltpu.VMEM((2, chunk, LANES), BF16),
            every,
            every,
            every,
            every,
            pltpu.VMEM((n_seq * chunk, LANES), F32),
            pltpu.VMEM((2, rows, width), BF16),
            pltpu.VMEM((2, rows, width), BF16),
            pltpu.VMEM((2 * part, LANES), F32),
            pltpu.VMEM((2 * part, LANES), F32),
            pltpu.VMEM((2 * PARTS, part, LANES), F32),
            pltpu.VMEM((2 * PARTS, n_seq, chunk // PARTS, LANES), BF16),
            pltpu.VMEM((2 * PARTS, n_seq, chunk // PARTS, LANES), BF16),
            pltpu.SemaphoreType.DMA((2, n_fsdp + n_fsdp // 2)),
            pltpu.SemaphoreType.DMA((2, n_fsdp)),
            pltpu.SemaphoreType.DMA((2, n_seq)),
            pltpu.SemaphoreType.DMA((2, n_seq)),
            pltpu.SemaphoreType.DMA((2,)),
            pltpu.SemaphoreType.DMA((2,)),
            pltpu.SemaphoreType.DMA((2 * PARTS,)),
            pltpu.SemaphoreType.DMA((2 * PARTS,)),
            pltpu.SemaphoreType.DMA((2 * PARTS, n_seq)),
            pltpu.SemaphoreType.DMA((2 * PARTS, n_seq)),
        ],
        compiler_params=pltpu.CompilerParams(
            collective_id=0, has_side_effects=True, vmem_limit_bytes=56 * 1024 * 1024
        ),
    )(table, inputs, out_grad, first_tiles, second_tiles)


def solution(mesh):
    placed = (
        P(("fsdp", "seq"), None),
        P(("fsdp", "seq"), None),
        P("seq", "fsdp", None),
        P("seq", None),
        P("seq", None),
        P("seq", "fsdp", None),
        P("seq", None),
        P("seq", None),
    )
    return jax.shard_map(
        functools.partial(on_device, mesh.shape["fsdp"], mesh.shape["seq"]),
        mesh=mesh,
        in_specs=placed,
        out_specs=(P(("fsdp", "seq"), None), P(("fsdp", "seq"), None)),
        check_vma=False,
    )
```

```python
import functools

import jax
import jax.numpy as jnp
from jax import lax
from jax.experimental import pallas as pl
from jax.experimental.pallas import tpu as pltpu
from jax.sharding import PartitionSpec as P

BS = 64
HB_DEV = 8
HALF = BS // 2
PARTS = 3
LANES = 128
MESH = pl.DeviceIdType.MESH
F32 = jnp.float32
BF16 = jnp.bfloat16


def gelu_pair(hidden):
    inner = 0.7978845608 * (hidden + 0.044715 * hidden * hidden * hidden)
    tangent = jnp.tanh(inner)
    value = 0.5 * hidden * (1.0 + tangent)
    slope = 0.5 * (1.0 + tangent) + 0.5 * hidden * (1.0 - tangent * tangent) * 0.7978845608 * (
        1.0 + 3.0 * 0.044715 * hidden * hidden
    )
    return (value, slope)


def block_slots(counts, blocks, capacity, number):
    shards = counts.shape[1]
    kept = blocks.shape[1]
    zero = shards * capacity
    shard = jnp.arange(shards, dtype=jnp.int32)
    ends = jnp.sum(jnp.where(shard[:, None] <= shard[None, :], counts[:, :, None], 0), axis=1)
    entry = jnp.arange(kept, dtype=jnp.int32)
    past = entry[None, :, None] >= ends[:, None, :]
    slot = entry[None, :] + jnp.sum(jnp.where(past, capacity - counts[:, None, :], 0), axis=2)
    block = jnp.arange(number, dtype=jnp.int32)
    same = blocks[:, None, :] == block[None, :, None]
    return zero + jnp.sum(jnp.where(same, slot[:, None, :] - zero, 0), axis=2)


def natural(position):
    within = position % BS
    return position - within + 2 * (within % HALF) + within // HALF


def kernel(
    n_fsdp,
    n_seq,
    slots_ref,
    x_ref,
    g_ref,
    one_ref,
    two_ref,
    out_ref,
    grad_ref,
    tiles_one,
    tiles_two,
    stage,
    first,
    second,
    got_x,
    got_g,
    pair_x,
    pair_g,
    spread,
    mat_x,
    mat_g,
    sums_a,
    sums_b,
    pair_sums,
    send_sums,
    half_sums,
    both_sums,
    got_sums,
    tile_send,
    tile_recv,
    row_send,
    row_recv,
    share_send,
    share_recv,
    join_send,
    join_recv,
    half_send,
    half_recv,
    sum_send,
    sum_recv,
):
    capacity = one_ref.shape[1]
    own, width = x_ref.shape
    groups = width // LANES
    rows = own * n_seq
    chunk = own * groups
    width_blocks = width // BS
    mine = HB_DEV // 2
    hid = mine * BS
    part_groups = groups // PARTS
    part_rows = rows * part_groups
    zero_slot = n_fsdp * capacity
    f = lax.axis_index("fsdp")
    s = lax.axis_index("seq")
    core = lax.rem(f, 2)
    pair = f + 1 - 2 * core
    others = [lax.rem(f + 2 * j, n_fsdp) for j in range(1, n_fsdp // 2)]
    pair_others = [lax.rem(pair + 2 * j, n_fsdp) for j in range(1, n_fsdp // 2)]
    ranks = n_seq // 2
    side = lax.rem(s, 2)
    rank = s // 2
    mate = s + 1 - 2 * side
    far_ranks = [lax.rem(rank + j, ranks) for j in range(1, ranks)]
    far = [2 * other + side for other in far_ranks]

    barrier = pltpu.get_barrier_semaphore()
    for peer in [pair] + others:
        pl.semaphore_signal(barrier, inc=1, device_id=(peer, s), device_id_type=MESH)
    for peer in [mate] + far:
        pl.semaphore_signal(barrier, inc=1, device_id=(f, peer), device_id_type=MESH)

    def lay_tiles(source, target):
        for j in range(HALF):
            piece = source[0, :, j * LANES:(j + 1) * LANES].astype(F32)
            stage[pl.ds(j, capacity, stride=HALF), :] = piece
        target[pl.ds(f * capacity, capacity)] = (
            stage[0:capacity * HALF, :].astype(BF16).reshape(capacity, HALF, LANES)
        )
        target[zero_slot] = jnp.zeros((HALF, LANES), BF16)

    def tile_copy(which, buffer, owner, target, sem):
        part = buffer.at[pl.ds(owner * capacity, capacity)]
        return pltpu.make_async_remote_copy(
            src_ref=part,
            dst_ref=part,
            send_sem=tile_send.at[which, sem],
            recv_sem=tile_recv.at[which, owner],
            device_id=(target, s),
            device_id_type=MESH,
        )

    def place(owner_side, owner_rank):
        return owner_side * ranks + owner_rank

    def row_copy(which, got, slot, target, sem):
        return pltpu.make_async_remote_copy(
            src_ref=got.at[slot],
            dst_ref=got.at[slot],
            send_sem=row_send.at[which, sem],
            recv_sem=row_recv.at[which, slot],
            device_id=(f, target),
            device_id_type=MESH,
        )

    def half_copy(turn):
        return pltpu.make_async_remote_copy(
            src_ref=send_sums.at[turn, pl.ds((1 - side) * ranks, ranks)],
            dst_ref=half_sums.at[turn],
            send_sem=half_send.at[turn],
            recv_sem=half_recv.at[turn],
            device_id=(f, mate),
            device_id_type=MESH,
        )

    def sum_copy(turn, owner, target, sem):
        return pltpu.make_async_remote_copy(
            src_ref=both_sums.at[turn, target],
            dst_ref=got_sums.at[turn, owner],
            send_sem=sum_send.at[turn, sem],
            recv_sem=sum_recv.at[turn, owner],
            device_id=(f, 2 * target + side),
            device_id_type=MESH,
        )

    def share_copy(which, source, target):
        return pltpu.make_async_remote_copy(
            src_ref=source,
            dst_ref=target,
            send_sem=share_send.at[which],
            recv_sem=share_recv.at[which],
            device_id=(pair, s),
            device_id_type=MESH,
        )

    def join_copy(turn):
        return pltpu.make_async_remote_copy(
            src_ref=(sums_a, sums_b)[turn % 2].at[pl.ds(part_rows, part_rows)],
            dst_ref=pair_sums.at[turn],
            send_sem=join_send.at[turn],
            recv_sem=join_recv.at[turn],
            device_id=(pair, s),
            device_id_type=MESH,
        )

    sent = []

    def start(copy):
        copy.start()
        sent.append(copy)

    position = lax.broadcasted_iota(jnp.int32, (LANES, LANES), 1)
    row = lax.broadcasted_iota(jnp.int32, (LANES, LANES), 0)
    to_halves = jnp.where(natural(position) == row, 1.0, 0.0).astype(BF16)
    from_halves = jnp.where(natural(row) == position, 1.0, 0.0).astype(BF16)

    lay_tiles(one_ref, tiles_one)
    pl.semaphore_wait(barrier, 2 + len(others) + len(far))
    for j, peer in enumerate(others):
        start(tile_copy(0, tiles_one, f, peer, j))

    def lay_rows(source):
        for k in range(groups):
            piece = source[:, k * LANES:(k + 1) * LANES].astype(F32)
            stage[pl.ds(k, own, stride=groups), :] = piece
        return stage[0:chunk, :].astype(BF16)

    here = place(side, rank)

    def send_rows(which, got):
        for j, peer in enumerate(far):
            start(row_copy(which, got, here, peer, j))
        start(row_copy(which, got, here, mate, ranks))

    def relay_rows(which, got):
        for j, other in enumerate(far_ranks):
            row_copy(which, got, place(side, other), mate, 0).wait_recv()
            start(row_copy(which, got, place(side, other), mate, ranks + 1 + j))

    got_x[here] = jnp.dot(lay_rows(x_ref), to_halves, preferred_element_type=F32).astype(BF16)
    send_rows(0, got_x)
    start(tile_copy(0, tiles_one, f, pair, n_fsdp))
    lay_tiles(two_ref, tiles_two)
    for j, peer in enumerate(others):
        start(tile_copy(1, tiles_two, f, peer, j))
    got_g[here] = lay_rows(g_ref)
    send_rows(1, got_g)
    start(tile_copy(1, tiles_two, f, pair, n_fsdp))

    def collect_rows(which, got, shared, mat):
        for other in [rank] + far_ranks:
            row_copy(which, got, place(1 - side, other), mate, 0).wait_recv()
        start(share_copy(which, got, shared))
        for half, source in enumerate((got, shared)):
            if half == 1:
                share_copy(which, got, shared).wait_recv()
            spread[...] = source[...].reshape(n_seq * chunk, LANES).astype(F32)
            for k in range(groups):
                piece = spread[pl.ds(k, rows, stride=groups), :]
                mat[half, :, k * LANES:(k + 1) * LANES] = piece.astype(BF16)

    def rows_of(mat, at):
        return jnp.concatenate([mat[0, :, at], mat[1, :, at]], axis=0)

    def collect_tiles(which, buffer):
        for j, peer in enumerate(others):
            tile_copy(which, buffer, peer, pair, 0).wait_recv()
            start(tile_copy(which, buffer, peer, pair, n_fsdp + 1 + j))
        tile_copy(which, buffer, pair, pair, 0).wait_recv()
        for peer in pair_others:
            tile_copy(which, buffer, peer, pair, 0).wait_recv()

    def joined(buffer, left, right):
        a = buffer[left]
        b = buffer[right]
        even = jnp.concatenate([a[:, :BS], b[:, :BS]], axis=1)
        odd = jnp.concatenate([a[:, BS:], b[:, BS:]], axis=1)
        return jnp.concatenate([even, odd], axis=0)

    relay_rows(0, got_x)
    relay_rows(1, got_g)
    collect_rows(0, got_x, pair_x, mat_x)
    collect_tiles(0, tiles_one)

    step = 4

    def build_first(i, total):
        for r in range(step):
            block = (i * step + r) * HB_DEV + core * mine
            at = pl.ds(pl.multiple_of((i * step + r) * BS, BS), BS)
            for j in range(mine // 2):
                tile = joined(
                    tiles_one, slots_ref[0, block + 2 * j], slots_ref[0, block + 2 * j + 1]
                )
                first[at, j * LANES:(j + 1) * LANES] = tile
        at = pl.ds(pl.multiple_of(i * (step * BS), step * BS), step * BS)
        return total + jnp.dot(rows_of(mat_x, at), first[at, :], preferred_element_type=F32)

    hidden = lax.fori_loop(
        0, width_blocks // step, build_first, jnp.zeros((2 * rows, hid), F32)
    )

    def reorder(value, matrix):
        parts = [
            jnp.dot(value[:, k * LANES:(k + 1) * LANES], matrix, preferred_element_type=F32)
            for k in range(hid // LANES)
        ]
        return jnp.concatenate(parts, axis=1)

    top = hidden.astype(BF16)
    rest = (hidden - top.astype(F32)).astype(BF16)
    hidden = reorder(top, to_halves) + reorder(rest, to_halves)
    value, slope = gelu_pair(hidden)
    acts = value.astype(BF16)

    collect_rows(1, got_g, pair_g, mat_g)
    collect_tiles(1, tiles_two)

    def pass_on(turn):
        join_copy(turn).wait_recv()
        kept = (sums_a, sums_b)[turn % 2][0:part_rows, :]
        total = (kept + pair_sums[turn]).astype(BF16)
        send_sums[turn] = total.reshape(n_seq, own * part_groups, LANES)
        start(half_copy(turn))

    def spread_sums(turn):
        half_copy(turn).wait_recv()
        kept = send_sums[turn, pl.ds(side * ranks, ranks)].astype(F32)
        both_sums[turn] = (kept + half_sums[turn].astype(F32)).astype(BF16)
        for j, other in enumerate(far_ranks):
            start(sum_copy(turn, rank, other, j))

    pairs = part_groups // 2

    def columns(part, i):
        return pl.ds(pl.multiple_of((part * pairs + i) * 2 * LANES, 2 * LANES), 2 * LANES)

    def put(turn, i, value):
        target = (sums_a, sums_b)[turn % 2]
        for k in range(2):
            at = pl.ds(2 * i + k, 2 * rows, stride=part_groups)
            target[at, :] = value[:, k * LANES:(k + 1) * LANES]

    back = jnp.zeros((2 * rows, hid), F32)
    for turn in range(PARTS):
        if turn >= 2:
            join_copy(turn - 2).wait_send()

        def build_second(i, total):
            for k in range(2):
                block = ((turn * pairs + i) * 2 + k) * 2
                at = pl.ds(pl.multiple_of(block * BS, LANES), LANES)
                for r in range(mine):
                    left = (core * mine + r) * width_blocks + block
                    tile = joined(tiles_two, slots_ref[1, left], slots_ref[1, left + 1])
                    second[r * BS:(r + 1) * BS, at] = tile
            at = columns(turn, i)
            weight = second[:, at]
            put(turn, i, jnp.dot(acts, weight, preferred_element_type=F32))
            return total + lax.dot_general(
                rows_of(mat_g, at),
                weight,
                (((1,), (1,)), ((), ())),
                preferred_element_type=F32,
            )

        back = lax.fori_loop(0, pairs, build_second, back)
        join_copy(turn).start()
        if turn >= 1:
            pass_on(turn - 1)
        if turn >= 2:
            spread_sums(turn - 2)

    pre = (back * slope).astype(BF16)
    pre = reorder(pre, from_halves).astype(BF16)
    pass_on(PARTS - 1)
    spread_sums(PARTS - 2)

    for turn in range(PARTS, 2 * PARTS):
        join_copy(turn - 2).wait_send()

        def in_grad(i, carry):
            part = lax.dot_general(
                pre,
                first[columns(turn - PARTS, i), :],
                (((1,), (1,)), ((), ())),
                preferred_element_type=F32,
            )
            put(turn, i, part)
            return carry

        lax.fori_loop(0, pairs, in_grad, 0)
        join_copy(turn).start()
        if turn > PARTS:
            pass_on(turn - 1)
            spread_sums(turn - 2)
    pass_on(2 * PARTS - 1)
    spread_sums(2 * PARTS - 2)
    spread_sums(2 * PARTS - 1)

    part_chunk = own * part_groups
    for turn in range(2 * PARTS):
        total = both_sums[turn, rank].astype(F32)
        for other in far_ranks:
            sum_copy(turn, other, other, 0).wait_recv()
            total = total + got_sums[turn, other].astype(F32)
        if turn >= PARTS:
            total = jnp.dot(total.astype(BF16), from_halves, preferred_element_type=F32)
        stage[0:part_chunk, :] = total
        target = out_ref if turn < PARTS else grad_ref
        for k in range(part_groups):
            piece = stage[pl.ds(k, own, stride=part_groups), :]
            column = (turn % PARTS) * part_groups + k
            target[:, column * LANES:(column + 1) * LANES] = piece.astype(BF16)
    for turn in range(2 * PARTS - 2, 2 * PARTS):
        join_copy(turn).wait_send()
    for copy in sent:
        copy.wait_send()


def on_device(
    n_fsdp,
    n_seq,
    inputs,
    out_grad,
    first_tiles,
    first_count,
    first_blocks,
    second_tiles,
    second_count,
    second_blocks,
):
    own, width = inputs.shape
    capacity = first_tiles.shape[1]
    width_blocks = width // BS
    rows = own * n_seq
    chunk = own * (width // LANES)
    hid = HB_DEV // 2 * BS
    part = rows * (width // LANES) // PARTS
    table = block_slots(
        jnp.concatenate([first_count, second_count]),
        jnp.concatenate([first_blocks, second_blocks]),
        capacity,
        width_blocks * HB_DEV,
    )
    vmem = pl.BlockSpec(memory_space=pltpu.VMEM)
    bank = pltpu.VMEM((n_fsdp * capacity + 1, HALF, LANES), BF16)
    some = pltpu.VMEM((2 * PARTS, n_seq // 2, chunk // PARTS, LANES), BF16)
    every = pltpu.VMEM((n_seq, chunk, LANES), BF16)
    return pl.pallas_call(
        functools.partial(kernel, n_fsdp, n_seq),
        out_shape=(
            jax.ShapeDtypeStruct((own, width), BF16),
            jax.ShapeDtypeStruct((own, width), BF16),
        ),
        in_specs=[pl.BlockSpec(memory_space=pltpu.SMEM)] + [vmem] * 4,
        out_specs=(vmem, vmem),
        scratch_shapes=[
            bank,
            bank,
            pltpu.VMEM((max(capacity * HALF, chunk), LANES), F32),
            pltpu.VMEM((width, hid), BF16),
            pltpu.VMEM((hid, width), BF16),
            every,
            every,
            every,
            every,
            pltpu.VMEM((n_seq * chunk, LANES), F32),
            pltpu.VMEM((2, rows, width), BF16),
            pltpu.VMEM((2, rows, width), BF16),
            pltpu.VMEM((2 * part, LANES), F32),
            pltpu.VMEM((2 * part, LANES), F32),
            pltpu.VMEM((2 * PARTS, part, LANES), F32),
            pltpu.VMEM((2 * PARTS, n_seq, chunk // PARTS, LANES), BF16),
            some,
            some,
            some,
            pltpu.SemaphoreType.DMA((2, n_fsdp + n_fsdp // 2)),
            pltpu.SemaphoreType.DMA((2, n_fsdp)),
            pltpu.SemaphoreType.DMA((2, n_seq)),
            pltpu.SemaphoreType.DMA((2, n_seq)),
            pltpu.SemaphoreType.DMA((2,)),
            pltpu.SemaphoreType.DMA((2,)),
            pltpu.SemaphoreType.DMA((2 * PARTS,)),
            pltpu.SemaphoreType.DMA((2 * PARTS,)),
            pltpu.SemaphoreType.DMA((2 * PARTS,)),
            pltpu.SemaphoreType.DMA((2 * PARTS,)),
            pltpu.SemaphoreType.DMA((2 * PARTS, n_seq // 2)),
            pltpu.SemaphoreType.DMA((2 * PARTS, n_seq // 2)),
        ],
        compiler_params=pltpu.CompilerParams(
            collective_id=0, has_side_effects=True, vmem_limit_bytes=56 * 1024 * 1024
        ),
    )(table, inputs, out_grad, first_tiles, second_tiles)


def solution(mesh):
    placed = (
        P(("fsdp", "seq"), None),
        P(("fsdp", "seq"), None),
        P("seq", "fsdp", None),
        P("seq", None),
        P("seq", None),
        P("seq", "fsdp", None),
        P("seq", None),
        P("seq", None),
    )
    return jax.shard_map(
        functools.partial(on_device, mesh.shape["fsdp"], mesh.shape["seq"]),
        mesh=mesh,
        in_specs=placed,
        out_specs=(P(("fsdp", "seq"), None), P(("fsdp", "seq"), None)),
        check_vma=False,
    )
```

```python
import functools

import jax
import jax.numpy as jnp
from jax import lax
from jax.experimental import pallas as pl
from jax.experimental.pallas import tpu as pltpu
from jax.sharding import PartitionSpec as P

BS = 64
HB_DEV = 8
HALF = BS // 2
PARTS = 3
LANES = 128
MESH = pl.DeviceIdType.MESH
F32 = jnp.float32
BF16 = jnp.bfloat16


def gelu_pair(hidden):
    inner = 0.7978845608 * (hidden + 0.044715 * hidden * hidden * hidden)
    tangent = jnp.tanh(inner)
    value = 0.5 * hidden * (1.0 + tangent)
    slope = 0.5 * (1.0 + tangent) + 0.5 * hidden * (1.0 - tangent * tangent) * 0.7978845608 * (
        1.0 + 3.0 * 0.044715 * hidden * hidden
    )
    return (value, slope)


def block_slots(counts, blocks, capacity, number):
    shards = counts.shape[1]
    kept = blocks.shape[1]
    zero = shards * capacity
    shard = jnp.arange(shards, dtype=jnp.int32)
    ends = jnp.sum(jnp.where(shard[:, None] <= shard[None, :], counts[:, :, None], 0), axis=1)
    entry = jnp.arange(kept, dtype=jnp.int32)
    past = entry[None, :, None] >= ends[:, None, :]
    slot = entry[None, :] + jnp.sum(jnp.where(past, capacity - counts[:, None, :], 0), axis=2)
    block = jnp.arange(number, dtype=jnp.int32)
    same = blocks[:, None, :] == block[None, :, None]
    return zero + jnp.sum(jnp.where(same, slot[:, None, :] - zero, 0), axis=2)


def natural(position):
    within = position % BS
    return position - within + 2 * (within % HALF) + within // HALF


def kernel(
    n_fsdp,
    n_seq,
    slots_ref,
    x_ref,
    g_ref,
    one_ref,
    two_ref,
    out_ref,
    grad_ref,
    tiles_one,
    tiles_two,
    stage,
    first,
    second,
    own_rows,
    got_x,
    got_g,
    spread,
    mat_x,
    mat_g,
    send_sums,
    got_sums,
    tile_send,
    tile_recv,
    row_send,
    row_recv,
    sum_send,
    sum_recv,
):
    capacity = one_ref.shape[1]
    own, width = x_ref.shape
    groups = width // LANES
    rows = own * n_seq
    chunk = own * groups
    width_blocks = width // BS
    hid = HB_DEV * BS
    part_groups = groups // PARTS
    part_chunk = own * part_groups
    part_rows = rows * part_groups
    pairs = part_groups // 2
    zero_slot = n_fsdp * capacity
    f = lax.axis_index("fsdp")
    s = lax.axis_index("seq")
    pair = f + 1 - 2 * lax.rem(f, 2)
    others = [lax.rem(f + 2 * j, n_fsdp) for j in range(1, n_fsdp // 2)]
    pair_others = [lax.rem(pair + 2 * j, n_fsdp) for j in range(1, n_fsdp // 2)]
    peers = [lax.rem(s + j, n_seq) for j in range(1, n_seq)]

    barrier = pltpu.get_barrier_semaphore()
    for peer in [pair] + others:
        pl.semaphore_signal(barrier, inc=1, device_id=(peer, s), device_id_type=MESH)
    for peer in peers:
        pl.semaphore_signal(barrier, inc=1, device_id=(f, peer), device_id_type=MESH)

    def lay_tiles(source, target):
        for j in range(HALF):
            piece = source[0, :, j * LANES:(j + 1) * LANES].astype(F32)
            stage[pl.ds(j, capacity, stride=HALF), :] = piece
        target[pl.ds(f * capacity, capacity)] = (
            stage[0:capacity * HALF, :].astype(BF16).reshape(capacity, HALF, LANES)
        )
        target[zero_slot] = jnp.zeros((HALF, LANES), BF16)

    def tile_copy(which, buffer, owner, target, sem):
        part = buffer.at[pl.ds(owner * capacity, capacity)]
        return pltpu.make_async_remote_copy(
            src_ref=part,
            dst_ref=part,
            send_sem=tile_send.at[which, sem],
            recv_sem=tile_recv.at[which, owner],
            device_id=(target, s),
            device_id_type=MESH,
        )

    def row_copy(which, source, got, owner, target, sem):
        return pltpu.make_async_remote_copy(
            src_ref=source,
            dst_ref=got.at[owner],
            send_sem=row_send.at[which, sem],
            recv_sem=row_recv.at[which, owner],
            device_id=(f, target),
            device_id_type=MESH,
        )

    def sum_copy(turn, owner, target, sem):
        return pltpu.make_async_remote_copy(
            src_ref=send_sums.at[turn, target],
            dst_ref=got_sums.at[turn, owner],
            send_sem=sum_send.at[turn, sem],
            recv_sem=sum_recv.at[turn, owner],
            device_id=(f, target),
            device_id_type=MESH,
        )

    sent = []

    def start(copy):
        copy.start()
        sent.append(copy)

    position = lax.broadcasted_iota(jnp.int32, (LANES, LANES), 1)
    row = lax.broadcasted_iota(jnp.int32, (LANES, LANES), 0)
    to_halves = jnp.where(natural(position) == row, 1.0, 0.0).astype(BF16)
    from_halves = jnp.where(natural(row) == position, 1.0, 0.0).astype(BF16)

    lay_tiles(one_ref, tiles_one)
    pl.semaphore_wait(barrier, 1 + len(others) + len(peers))
    for j, peer in enumerate(others):
        start(tile_copy(0, tiles_one, f, peer, j))

    def lay_rows(source):
        for k in range(groups):
            piece = source[:, k * LANES:(k + 1) * LANES].astype(F32)
            stage[pl.ds(k, own, stride=groups), :] = piece
        return stage[0:chunk, :].astype(BF16)

    own_rows[0] = jnp.dot(lay_rows(x_ref), to_halves, preferred_element_type=F32).astype(BF16)
    for j, peer in enumerate(peers):
        start(row_copy(0, own_rows.at[0], got_x, s, peer, j))
    start(tile_copy(0, tiles_one, f, pair, n_fsdp))
    lay_tiles(two_ref, tiles_two)
    for j, peer in enumerate(others):
        start(tile_copy(1, tiles_two, f, peer, j))
    own_rows[1] = lay_rows(g_ref)
    for j, peer in enumerate(peers):
        start(row_copy(1, own_rows.at[1], got_g, s, peer, j))
    start(tile_copy(1, tiles_two, f, pair, n_fsdp))
    got_x[s] = own_rows[0]
    got_g[s] = own_rows[1]

    def collect_rows(which, got, mat):
        for peer in peers:
            row_copy(which, own_rows.at[which], got, peer, peer, 0).wait_recv()
        spread[...] = got[...].reshape(n_seq * chunk, LANES).astype(F32)
        for k in range(groups):
            piece = spread[pl.ds(k, rows, stride=groups), :]
            mat[:, k * LANES:(k + 1) * LANES] = piece.astype(BF16)

    def relay_tiles(which, buffer):
        for j, peer in enumerate(others):
            tile_copy(which, buffer, peer, pair, 0).wait_recv()
            start(tile_copy(which, buffer, peer, pair, n_fsdp + 1 + j))

    def collect_tiles(which, buffer):
        tile_copy(which, buffer, pair, pair, 0).wait_recv()
        for peer in pair_others:
            tile_copy(which, buffer, peer, pair, 0).wait_recv()

    def joined(buffer, left, right):
        a = buffer[left]
        b = buffer[right]
        even = jnp.concatenate([a[:, :BS], b[:, :BS]], axis=1)
        odd = jnp.concatenate([a[:, BS:], b[:, BS:]], axis=1)
        return jnp.concatenate([even, odd], axis=0)

    collect_rows(0, got_x, mat_x)
    relay_tiles(0, tiles_one)
    collect_tiles(0, tiles_one)

    step = 4

    def build_first(i, total):
        for r in range(step):
            block = (i * step + r) * HB_DEV
            at = pl.ds(pl.multiple_of((i * step + r) * BS, BS), BS)
            for j in range(HB_DEV // 2):
                tile = joined(
                    tiles_one, slots_ref[0, block + 2 * j], slots_ref[0, block + 2 * j + 1]
                )
                first[at, j * LANES:(j + 1) * LANES] = tile
        at = pl.ds(pl.multiple_of(i * (step * BS), step * BS), step * BS)
        return total + jnp.dot(mat_x[:, at], first[at, :], preferred_element_type=F32)

    hidden = lax.fori_loop(
        0, width_blocks // step, build_first, jnp.zeros((rows, hid), F32)
    )

    def reorder(value, matrix):
        parts = [
            jnp.dot(value[:, k * LANES:(k + 1) * LANES], matrix, preferred_element_type=F32)
            for k in range(hid // LANES)
        ]
        return jnp.concatenate(parts, axis=1)

    top = hidden.astype(BF16)
    rest = (hidden - top.astype(F32)).astype(BF16)
    hidden = reorder(top, to_halves) + reorder(rest, to_halves)
    value, slope = gelu_pair(hidden)
    acts = value.astype(BF16)

    relay_tiles(1, tiles_two)
    collect_rows(1, got_g, mat_g)
    collect_tiles(1, tiles_two)

    def put(i, value):
        for k in range(2):
            at = pl.ds(2 * i + k, rows, stride=part_groups)
            spread[at, :] = value[:, k * LANES:(k + 1) * LANES]

    def send_part(turn):
        total = spread[0:part_rows, :].astype(BF16)
        send_sums[turn] = total.reshape(n_seq, part_chunk, LANES)
        for j, peer in enumerate(peers):
            start(sum_copy(turn, s, peer, j))

    back = jnp.zeros((rows, hid), F32)
    for turn in range(PARTS):

        def build_second(i, total):
            n = turn * pairs + i
            for k in range(2):
                block = n * 4 + 2 * k
                at = pl.ds(pl.multiple_of((2 * n + k) * LANES, LANES), LANES)
                for r in range(HB_DEV):
                    left = r * width_blocks + block
                    tile = joined(tiles_two, slots_ref[1, left], slots_ref[1, left + 1])
                    second[r * BS:(r + 1) * BS, at] = tile
            at = pl.ds(pl.multiple_of(2 * n * LANES, 2 * LANES), 2 * LANES)
            weight = second[:, at]
            put(i, jnp.dot(acts, weight, preferred_element_type=F32))
            return total + lax.dot_general(
                mat_g[:, at], weight, (((1,), (1,)), ((), ())), preferred_element_type=F32
            )

        back = lax.fori_loop(0, pairs, build_second, back)
        send_part(turn)

    pre = (back * slope).astype(BF16)
    pre = reorder(pre, from_halves).astype(BF16)

    for turn in range(PARTS, 2 * PARTS):

        def in_grad(i, carry):
            n = (turn - PARTS) * pairs + i
            at = pl.ds(pl.multiple_of(2 * n * LANES, 2 * LANES), 2 * LANES)
            part = lax.dot_general(
                pre, first[at, :], (((1,), (1,)), ((), ())), preferred_element_type=F32
            )
            put(i, part)
            return carry

        lax.fori_loop(0, pairs, in_grad, 0)
        send_part(turn)

    for turn in range(2 * PARTS):
        total = send_sums[turn, s].astype(F32)
        for peer in peers:
            sum_copy(turn, peer, peer, 0).wait_recv()
            total = total + got_sums[turn, peer].astype(F32)
        if turn >= PARTS:
            total = jnp.dot(total.astype(BF16), from_halves, preferred_element_type=F32)
        stage[0:part_chunk, :] = total
        target = out_ref if turn < PARTS else grad_ref
        for k in range(part_groups):
            piece = stage[pl.ds(k, own, stride=part_groups), :]
            column = (turn % PARTS) * part_groups + k
            target[:, column * LANES:(column + 1) * LANES] = piece.astype(BF16)
    for copy in sent:
        copy.wait_send()


def on_device(
    n_fsdp,
    n_seq,
    inputs,
    out_grad,
    first_tiles,
    first_count,
    first_blocks,
    second_tiles,
    second_count,
    second_blocks,
):
    own, width = inputs.shape
    capacity = first_tiles.shape[1]
    width_blocks = width // BS
    rows = own * n_seq
    chunk = own * (width // LANES)
    hid = HB_DEV * BS
    table = block_slots(
        jnp.concatenate([first_count, second_count]),
        jnp.concatenate([first_blocks, second_blocks]),
        capacity,
        width_blocks * HB_DEV,
    )
    vmem = pl.BlockSpec(memory_space=pltpu.VMEM)
    bank = pltpu.VMEM((n_fsdp * capacity + 1, HALF, LANES), BF16)
    parts = pltpu.VMEM((2 * PARTS, n_seq, chunk // PARTS, LANES), BF16)
    every = pltpu.VMEM((n_seq, chunk, LANES), BF16)
    return pl.pallas_call(
        functools.partial(kernel, n_fsdp, n_seq),
        out_shape=(
            jax.ShapeDtypeStruct((own, width), BF16),
            jax.ShapeDtypeStruct((own, width), BF16),
        ),
        in_specs=[pl.BlockSpec(memory_space=pltpu.SMEM)] + [vmem] * 4,
        out_specs=(vmem, vmem),
        scratch_shapes=[
            bank,
            bank,
            pltpu.VMEM((max(capacity * HALF, chunk), LANES), F32),
            pltpu.VMEM((width, hid), BF16),
            pltpu.VMEM((hid, width), BF16),
            pltpu.VMEM((2, chunk, LANES), BF16),
            every,
            every,
            pltpu.VMEM((n_seq * chunk, LANES), F32),
            pltpu.VMEM((rows, width), BF16),
            pltpu.VMEM((rows, width), BF16),
            parts,
            parts,
            pltpu.SemaphoreType.DMA((2, n_fsdp + n_fsdp // 2)),
            pltpu.SemaphoreType.DMA((2, n_fsdp)),
            pltpu.SemaphoreType.DMA((2, n_seq)),
            pltpu.SemaphoreType.DMA((2, n_seq)),
            pltpu.SemaphoreType.DMA((2 * PARTS, n_seq)),
            pltpu.SemaphoreType.DMA((2 * PARTS, n_seq)),
        ],
        compiler_params=pltpu.CompilerParams(
            collective_id=0, has_side_effects=True, vmem_limit_bytes=56 * 1024 * 1024
        ),
    )(table, inputs, out_grad, first_tiles, second_tiles)


def solution(mesh):
    placed = (
        P(("fsdp", "seq"), None),
        P(("fsdp", "seq"), None),
        P("seq", "fsdp", None),
        P("seq", None),
        P("seq", None),
        P("seq", "fsdp", None),
        P("seq", None),
        P("seq", None),
    )
    return jax.shard_map(
        functools.partial(on_device, mesh.shape["fsdp"], mesh.shape["seq"]),
        mesh=mesh,
        in_specs=placed,
        out_specs=(P(("fsdp", "seq"), None), P(("fsdp", "seq"), None)),
        check_vma=False,
    )
```
